256 devices in a mesh: tiles: 64 (over z, x, core), pair: 4 (over y).
Axes of the slice: x: 4, y: 4, z: 8, core: 2. Of those that a mesh axis runs over, the one named last changes fastest.
Arguments:
- t2: bfloat16 [2048, 16, 4096], P('tiles', None, 'pair'), may hold values from -6 to 6
- v_plus: bfloat16 [64, 64, 16, 2048], P('tiles'), may hold values from -0.1875 to 0.1875
- v_minus: bfloat16 [64, 64, 16, 2048], P('tiles'), may hold values from -0.1875 to 0.1875
- partner: int32 [4096], P('pair'), may hold values from 0 to 1023, as said below
- win_tile: int32 [64, 64], replicated, may hold values from 0 to 2047, as said below
- win_count: int32 [64], replicated, may hold values from 48 to 64, as said below
Outputs:
- ladder: bfloat16 [4096, 131072], P('pair', 'tiles')
The draws below stay inside these ranges and needn't reach their ends.
Inputs may be any that keep to these rules, and one draw needn't show every extreme that they name: `partner`: each block of 1024 entries is a permutation of 0 to 1023, and blocks 2h and 2h + 1 are inverse to each other. `win_tile`: the live entries of one owner's list name distinct tiles; at most 2 of them lie among one index of tiles' 32 tiles (tiles k * 32 to (k + 1) * 32 - 1), and some owner takes exactly 2 from one index in every draw. Entries past the live count name tiles too. `win_count`: some owner has exactly 64 live slots.
All inputs are finite; a program needn't handle non-finite values.
Results may differ from the reference program's by a relative error of at most 0.0052.
Values may be sent and summed in bfloat16 or wider, within the bound.
No kernel may reach another device: no remote copies, remote signals or barrier semaphores. Data moves between devices by JAX's collectives and lax.ppermute only.
A program may use at most 128 MiB of HBM per device.

```python
import jax
import jax.numpy as jnp
from jax import lax

OP_DEV = 1024
TW = 16
WIN = 64
SAB = 2048
TILES_IN = 32
CAP = 2
NT = 2048
OPAIRS = 4096
N_TILES = 64
N_PAIR = 4


def window_lists(key):
    key_count, key_second, key_order, key_full, key_shuffle, key_start = jax.random.split(key, 6)
    span_size = WIN // 4
    first_draw = jax.random.randint(key_count, (N_TILES,), 0, span_size + 1)
    second_draw = jax.random.randint(key_second, (N_TILES,), 0, span_size + 1)
    counts = WIN - jnp.minimum(first_draw, second_draw)
    full_owner = jax.random.randint(key_full, (), 0, N_TILES)
    counts = jnp.where(jnp.arange(N_TILES) == full_owner, WIN, counts).astype(jnp.int32)
    source_orders = jax.vmap(lambda k: jax.random.permutation(k, N_TILES))(jax.random.split(key_order, N_TILES))
    start_tiles = jax.random.randint(key_start, (N_TILES, N_TILES), 0, TILES_IN)
    slot_block = jnp.arange(WIN) // CAP
    in_block = jnp.arange(WIN) % CAP
    sources = source_orders[:, slot_block]
    offsets = (start_tiles[:, slot_block] + in_block[None, :]) % TILES_IN
    tiles = sources * TILES_IN + offsets
    scores = jax.random.randint(key_shuffle, (N_TILES, WIN), 0, 4096) * WIN + jnp.arange(WIN)[None, :]
    scores = scores + jnp.where(jnp.arange(WIN)[None, :] < counts[:, None], 0, 2 ** 24)
    shuffle = jnp.argsort(scores, axis=1)
    tiles = jnp.take_along_axis(tiles, shuffle, axis=1)
    return (tiles.astype(jnp.int32), counts)


def draw_win_tile(key, part):
    return window_lists(key)[0]


def draw_win_count(key, part):
    return window_lists(key)[1]


def draw_partner(key, part):
    key = jax.random.fold_in(key, 7)
    half_count = N_PAIR // 2
    orders = jax.vmap(lambda k: jax.random.permutation(k, OP_DEV))(jax.random.split(key, half_count))
    inverse = jnp.argsort(orders, axis=1)
    stacked = jnp.stack([orders, inverse], axis=1)
    return stacked.reshape(half_count * 2 * OP_DEV).astype(jnp.int32)


def shard_levels(own_key, dims, pieces, low, top_value):
    def one(dim, shards_of):
        draws = jax.random.uniform(jax.random.fold_in(jax.random.fold_in(own_key, 6), dim), (shards_of,), jnp.float32, low / len(pieces), top_value / len(pieces))
        return jnp.repeat(jnp.exp(draws), dims[dim] // shards_of).reshape((-1,) + (1,) * (len(dims) - dim - 1))

    loudness = one(*pieces[0])
    for cut in pieces[1:]:
        loudness = loudness * one(*cut)
    return loudness


def bell_draw(rng, extent, scale, reach, cuts=(), held_as=jnp.bfloat16):
    entries = jax.random.normal(rng, extent, jnp.float32) * scale
    if len(cuts) > 0:
        entries = shard_levels(rng, extent, cuts, -0.22, 0.18) * entries
    return jnp.clip(entries, min=-reach, max=reach).astype(held_as)


def setup_inputs(seed: int = 0) -> dict:
    streams_of = jax.random.split(jax.random.key(seed), 7)
    t2 = bell_draw(streams_of[0], (NT, TW, OPAIRS), 1.0, 6.0, ((0, 64), (2, 4)))
    v_plus = bell_draw(streams_of[1], (N_TILES, WIN, TW, SAB), (WIN * TW) ** -0.5, 0.1875, ((0, 64),))
    v_minus = bell_draw(streams_of[2], (N_TILES, WIN, TW, SAB), (WIN * TW) ** -0.5, 0.1875, ((0, 64),))
    partner = draw_partner(jax.random.fold_in(streams_of[6], 71), 0)
    win_tile = draw_win_tile(jax.random.fold_in(streams_of[6], 71), 0)
    win_count = draw_win_count(jax.random.fold_in(streams_of[6], 71), 0)
    return {"t2": t2, "v_plus": v_plus, "v_minus": v_minus, "partner": partner, "win_tile": win_tile, "win_count": win_count}


def reference(t2, v_plus, v_minus, partner, win_tile, win_count):
    pair_rows = t2.shape[2]
    block_rows = pair_rows // N_PAIR
    block_id = (jnp.arange(pair_rows) // block_rows).astype(jnp.int32)
    mirror = (jnp.bitwise_xor(block_id, 1) * block_rows + partner).astype(jnp.int32)
    own_values = t2.astype(jnp.float32)
    mirror_values = jnp.take(t2, mirror, axis=2).astype(jnp.float32)
    plus = (own_values + mirror_values).astype(jnp.bfloat16)
    minus = (own_values - mirror_values).astype(jnp.bfloat16)
    contract = (((0, 1), (0, 1)), ((), ()))

    def owner_block(inputs):
        tiles_here, count_here, plus_slab, minus_slab = inputs
        living = (jnp.arange(WIN) < count_here)[:, None, None]
        wplus = jnp.where(living, jnp.take(plus, tiles_here, axis=0), jnp.zeros((), jnp.bfloat16))
        wminus = jnp.where(living, jnp.take(minus, tiles_here, axis=0), jnp.zeros((), jnp.bfloat16))
        first = lax.dot_general(wplus.astype(jnp.float32), plus_slab.astype(jnp.float32), contract)
        second = lax.dot_general(wminus.astype(jnp.float32), minus_slab.astype(jnp.float32), contract)
        return (0.5 * (first + second)).astype(jnp.bfloat16)

    blocks = lax.map(owner_block, (win_tile, win_count, v_plus, v_minus))
    return jnp.transpose(blocks, (1, 0, 2)).reshape(pair_rows, N_TILES * SAB)
```

```python
import functools

import jax
import jax.numpy as jnp
from jax import lax
from jax.experimental import pallas as pl
from jax.experimental.pallas import tpu as pltpu
from jax.sharding import PartitionSpec as P

CHUNKS = (640, 256, 128)
VMEM_LIMIT = 20 * 1024 * 1024


def mirror_pair(x):
    return lax.ppermute(x, "pair", [(i, i ^ 1) for i in range(lax.axis_size("pair"))])


def whole(count):
    return [pl.BlockSpec(memory_space=pltpu.VMEM)] * count


def scalars():
    return [pl.BlockSpec(memory_space=pltpu.SMEM)]


def params():
    return pltpu.CompilerParams(vmem_limit_bytes=VMEM_LIMIT)


def pack_kernel(table_ref, tiles_ref, out_ref):
    for k in range(out_ref.shape[0]):
        out_ref[k] = tiles_ref[table_ref[k]]


def pack(table, tiles):
    count = table.shape[0]
    return pl.pallas_call(
        pack_kernel,
        out_shape=jax.ShapeDtypeStruct((count,) + tiles.shape[1:], tiles.dtype),
        in_specs=scalars() + whole(1),
        out_specs=whole(1)[0],
        compiler_params=params(),
    )(table, tiles)


def window_kernel(where_ref, received_ref, out_ref):
    for w in range(out_ref.shape[0]):
        place = where_ref[w]
        tile = received_ref[jnp.maximum(place, 0)]
        out_ref[w] = jnp.where(place >= 0, tile, jnp.zeros_like(tile))


def unpack(where, received):
    return pl.pallas_call(
        window_kernel,
        out_shape=jax.ShapeDtypeStruct(where.shape + received.shape[1:], received.dtype),
        in_specs=scalars() + whole(1),
        out_specs=whole(1)[0],
        compiler_params=params(),
    )(where, received)


def ladder_kernel(first, block, *refs):
    own_ref, mirror_ref, restore_ref, plus_ref, minus_ref = refs[:5]
    base_ref = None if first else refs[5]
    out_ref = refs[5 if first else 6]
    slots, tile_width, width = own_ref.shape
    depth = slots * tile_width
    own = own_ref[...].reshape(depth, width).astype(jnp.float32)
    mirrored = mirror_ref[...].reshape(depth, width).astype(jnp.float32)
    plus = (own + mirrored).astype(jnp.bfloat16).T
    minus = (own - mirrored).astype(jnp.bfloat16).T
    restore = restore_ref[...]
    for begin in range(0, out_ref.shape[1], block):
        across = slice(begin, begin + block)
        total = jnp.dot(
            plus,
            plus_ref[:, :, across].reshape(depth, block),
            preferred_element_type=jnp.float32,
        )
        total = total + jnp.dot(
            minus,
            minus_ref[:, :, across].reshape(depth, block),
            preferred_element_type=jnp.float32,
        )
        ladder = jnp.dot(
            restore, (0.5 * total).astype(jnp.bfloat16), preferred_element_type=jnp.float32
        )
        if not first:
            ladder = ladder + base_ref[:, across].astype(jnp.float32)
        out_ref[:, across] = ladder.astype(out_ref.dtype)


def add_rows(own, mirrored, restore, plus_slab, minus_slab, base, block=512):
    slots, tile_width, width = own.shape
    columns = plus_slab.shape[2]
    rows = restore.shape[0]
    first = base is None
    return pl.pallas_call(
        functools.partial(ladder_kernel, first, block),
        out_shape=jax.ShapeDtypeStruct((rows, columns), jnp.bfloat16),
        in_specs=whole(5 if first else 6),
        out_specs=whole(1)[0],
        compiler_params=params(),
        cost_estimate=pl.CostEstimate(
            flops=4 * slots * tile_width * width * columns + 2 * rows * width * columns,
            bytes_accessed=4 * slots * tile_width * columns + 4 * rows * columns,
            transcendentals=0,
        ),
    )(own, mirrored, restore, plus_slab, minus_slab, *([] if first else [base]))


def route_plan(win_tile, win_count, me):
    slots = win_tile.shape[1]
    position = jnp.arange(slots)
    sources = win_tile >> 5
    mine = (sources == me) & (position[None, :] < win_count[:, None])
    coded = position[None, :] * 32 + (win_tile & 31)
    first = jnp.min(jnp.where(mine, coded, 1 << 20), axis=1) & 31
    last = jnp.maximum(jnp.max(jnp.where(mine, coded, -1), axis=1), 0) & 31
    send = jnp.stack([first, last], axis=1).reshape(-1)
    own = lax.dynamic_index_in_dim(sources, me, 0, keepdims=False)
    living = position < lax.dynamic_index_in_dim(win_count, me, 0, keepdims=False)
    earlier = (
        (own[:, None] == own[None, :])
        & living[None, :]
        & (position[None, :] < position[:, None])
    )
    rank = jnp.any(earlier, axis=1).astype(jnp.int32)
    return send, jnp.where(living, own * 2 + rank, -1)


def after(value, *others):
    return lax.optimization_barrier((value,) + others)[0]


def body(t2, v_plus, v_minus, partner, win_tile, win_count):
    tiles, tile_width, rows = t2.shape
    me = lax.axis_index("tiles")
    odd = lax.axis_index("pair") % 2 == 1
    index = jnp.arange(rows)
    order = jnp.where(odd, partner, index)
    send, where = route_plan(win_tile, win_count, me)
    flat = t2.reshape(tiles * tile_width, rows)
    ladder = None
    begin = 0
    windows = []
    for width in CHUNKS:
        select = (order[:, None] == index[None, begin : begin + width]).astype(jnp.bfloat16)
        chunk = jnp.dot(flat, select, preferred_element_type=jnp.float32).astype(jnp.bfloat16)
        outgoing = pack(send, chunk.reshape(tiles, tile_width, width))
        if windows:
            outgoing = after(outgoing, received)
        received = lax.all_to_all(outgoing, "tiles", 0, 0, tiled=True)
        windows.append((received, begin, width))
        begin += width
    for received, begin, width in windows:
        own = unpack(where, received)
        mirrored = mirror_pair(own)
        restore = (order[:, None] == index[None, begin : begin + width]).astype(jnp.bfloat16)
        ladder = add_rows(own, mirrored, restore, v_plus[0], v_minus[0], ladder)
    return ladder


def solution(mesh):
    placed = (
        P("tiles", None, "pair"),
        P("tiles", None, None, None),
        P("tiles", None, None, None),
        P("pair"),
        P(),
        P(),
    )
    return jax.shard_map(
        body, mesh=mesh, in_specs=placed, out_specs=P("pair", "tiles"), check_vma=False
    )
```

```python
import functools

import jax
import jax.numpy as jnp
from jax import lax
from jax.experimental import pallas as pl
from jax.experimental.pallas import tpu as pltpu
from jax.sharding import PartitionSpec as P

CHUNKS = ((512, 128), (256, 128))
BLOCK = 512
VMEM_LIMIT = 20 * 1024 * 1024


def mirror_pair(x):
    return lax.ppermute(x, "pair", [(i, i ^ 1) for i in range(lax.axis_size("pair"))])


def whole(count):
    return [pl.BlockSpec(memory_space=pltpu.VMEM)] * count


def scalars():
    return [pl.BlockSpec(memory_space=pltpu.SMEM)]


def params():
    return pltpu.CompilerParams(vmem_limit_bytes=VMEM_LIMIT)


def pack_kernel(table_ref, tiles_ref, out_ref):
    for k in range(out_ref.shape[0]):
        out_ref[k] = tiles_ref[table_ref[k]]


def pack(table, tiles):
    count = table.shape[0]
    return pl.pallas_call(
        pack_kernel,
        out_shape=jax.ShapeDtypeStruct((count,) + tiles.shape[1:], tiles.dtype),
        in_specs=scalars() + whole(1),
        out_specs=whole(1)[0],
        compiler_params=params(),
    )(table, tiles)


def window_kernel(begin, where_ref, received_ref, out_ref):
    width = out_ref.shape[2]
    for w in range(out_ref.shape[0]):
        place = where_ref[w]
        tile = received_ref[jnp.maximum(place, 0), :, begin : begin + width]
        out_ref[w] = jnp.where(place >= 0, tile, jnp.zeros_like(tile))


def unpack(where, received, begin, width):
    shape = where.shape + (received.shape[1], width)
    return pl.pallas_call(
        functools.partial(window_kernel, begin),
        out_shape=jax.ShapeDtypeStruct(shape, received.dtype),
        in_specs=scalars() + whole(1),
        out_specs=whole(1)[0],
        compiler_params=params(),
    )(where, received)


def turned_sums(own_ref, mirror_ref):
    slots, tile_width, width = own_ref.shape
    own = own_ref[...].reshape(slots * tile_width, width).astype(jnp.float32)
    mirrored = mirror_ref[...].reshape(slots * tile_width, width).astype(jnp.float32)
    plus = (own + mirrored).astype(jnp.bfloat16).T
    minus = (own - mirrored).astype(jnp.bfloat16).T
    return plus, minus


def product(plus, minus, plus_ref, minus_ref, across):
    depth = plus.shape[1]
    block = across.stop - across.start
    total = jnp.dot(
        plus, plus_ref[:, :, across].reshape(depth, block), preferred_element_type=jnp.float32
    )
    total = total + jnp.dot(
        minus, minus_ref[:, :, across].reshape(depth, block), preferred_element_type=jnp.float32
    )
    return (0.5 * total).astype(jnp.bfloat16)


def rows_kernel(own_ref, mirror_ref, plus_ref, minus_ref, out_ref):
    plus, minus = turned_sums(own_ref, mirror_ref)
    for begin in range(0, out_ref.shape[1], BLOCK):
        across = slice(begin, begin + BLOCK)
        out_ref[:, across] = product(plus, minus, plus_ref, minus_ref, across)


def cost(own, columns, more=0):
    depth = own.shape[0] * own.shape[1]
    return pl.CostEstimate(
        flops=4 * depth * own.shape[2] * columns + more,
        bytes_accessed=8 * depth * columns,
        transcendentals=0,
    )


def make_rows(own, mirrored, plus_slab, minus_slab):
    columns = plus_slab.shape[2]
    return pl.pallas_call(
        rows_kernel,
        out_shape=jax.ShapeDtypeStruct((own.shape[2], columns), jnp.bfloat16),
        in_specs=whole(4),
        out_specs=whole(1)[0],
        compiler_params=params(),
        cost_estimate=cost(own, columns),
    )(own, mirrored, plus_slab, minus_slab)


def finish_kernel(earlier, based, *refs):
    own_ref, mirror_ref, restore_ref, plus_ref, minus_ref = refs[:5]
    earlier_refs = refs[5 : 5 + earlier]
    refs = refs[5 + earlier :]
    if based:
        base_hbm, out_hbm, held, held_sems, based_on, base_sems = refs
    else:
        out_hbm, held, held_sems = refs
    blocks = range(held.shape[0])
    spans = [slice(b * BLOCK, b * BLOCK + BLOCK) for b in blocks]
    if based:
        loads = [
            pltpu.make_async_copy(base_hbm.at[:, spans[b]], based_on.at[b], base_sems.at[b])
            for b in blocks
        ]
        for load in loads:
            load.start()
    plus, minus = turned_sums(own_ref, mirror_ref)
    stores = []
    for b in blocks:
        parts = [ref[:, spans[b]] for ref in earlier_refs]
        parts.append(product(plus, minus, plus_ref, minus_ref, spans[b]))
        rows = parts[0] if len(parts) == 1 else jnp.concatenate(parts, axis=0)
        ladder = jnp.dot(restore_ref[...], rows, preferred_element_type=jnp.float32)
        if based:
            loads[b].wait()
            ladder = ladder + based_on[b].astype(jnp.float32)
        held[b] = ladder.astype(held.dtype)
        store = pltpu.make_async_copy(held.at[b], out_hbm.at[:, spans[b]], held_sems.at[b])
        store.start()
        stores.append(store)
    for store in stores:
        store.wait()


def finish(own, mirrored, restore, plus_slab, minus_slab, earlier, base):
    columns = plus_slab.shape[2]
    rows = restore.shape[0]
    blocks = columns // BLOCK
    in_hbm = pl.BlockSpec(memory_space=pltpu.HBM)
    held = [pltpu.VMEM((blocks, rows, BLOCK), jnp.bfloat16), pltpu.SemaphoreType.DMA((blocks,))]
    based = base is not None
    return pl.pallas_call(
        functools.partial(finish_kernel, len(earlier), based),
        out_shape=jax.ShapeDtypeStruct((rows, columns), jnp.bfloat16),
        in_specs=whole(5 + len(earlier)) + ([in_hbm] if based else []),
        out_specs=in_hbm,
        scratch_shapes=held * (2 if based else 1),
        compiler_params=params(),
        cost_estimate=cost(own, columns, 2 * rows * restore.shape[1] * columns),
    )(own, mirrored, restore, plus_slab, minus_slab, *earlier, *([base] if based else []))


def pin_kernel(slab_ref, out_ref, sem):
    copy = pltpu.make_async_copy(slab_ref, out_ref, sem)
    copy.start()
    copy.wait()


def pin(slab):
    return pl.pallas_call(
        pin_kernel,
        out_shape=pltpu.VMEM(slab.shape, slab.dtype),
        in_specs=[pl.BlockSpec(memory_space=pltpu.HBM)],
        out_specs=pl.BlockSpec(memory_space=pltpu.VMEM),
        scratch_shapes=[pltpu.SemaphoreType.DMA],
        compiler_params=params(),
    )(slab)


def route_plan(win_tile, win_count, me):
    slots = win_tile.shape[1]
    position = jnp.arange(slots)
    sources = win_tile >> 5
    mine = (sources == me) & (position[None, :] < win_count[:, None])
    coded = position[None, :] * 32 + (win_tile & 31)
    first = jnp.min(jnp.where(mine, coded, 1 << 20), axis=1) & 31
    last = jnp.maximum(jnp.max(jnp.where(mine, coded, -1), axis=1), 0) & 31
    send = jnp.stack([first, last], axis=1).reshape(-1)
    own = lax.dynamic_index_in_dim(sources, me, 0, keepdims=False)
    living = position < lax.dynamic_index_in_dim(win_count, me, 0, keepdims=False)
    earlier = (
        (own[:, None] == own[None, :])
        & living[None, :]
        & (position[None, :] < position[:, None])
    )
    rank = jnp.any(earlier, axis=1).astype(jnp.int32)
    return send, jnp.where(living, own * 2 + rank, -1)


def after(value, *others):
    return lax.optimization_barrier((value,) + others)[0]


def body(t2, v_plus, v_minus, partner, win_tile, win_count):
    tiles, tile_width, rows = t2.shape
    me = lax.axis_index("tiles")
    odd = lax.axis_index("pair") % 2 == 1
    index = jnp.arange(rows)
    order = jnp.where(odd, partner, index)
    send, where = route_plan(win_tile, win_count, me)
    flat = t2.reshape(tiles * tile_width, rows)
    begin = 0
    chunks, restores = [], []
    for pieces in CHUNKS:
        width = sum(pieces)
        select = (order[:, None] == index[None, begin : begin + width]).astype(jnp.bfloat16)
        chunk = jnp.dot(flat, select, preferred_element_type=jnp.float32).astype(jnp.bfloat16)
        chunks.append(chunk.reshape(tiles, tile_width, width))
        restores.append(select)
        begin += width
    landed = [lax.all_to_all(pack(send, chunks[0]), "tiles", 0, 0, tiled=True)]
    early = tuple(restores) + (where,) + tuple(chunks[1:])
    plus_slab = pin(after(v_plus[0], *early))
    minus_slab = pin(after(v_minus[0], *early))
    for chunk in chunks[1:]:
        outgoing = pack(send, after(chunk, plus_slab, minus_slab))
        outgoing = after(outgoing, landed[-1])
        landed.append(lax.all_to_all(outgoing, "tiles", 0, 0, tiled=True))
    ladder = None
    earlier = []
    for pieces, received, restore in zip(CHUNKS, landed, restores, strict=True):
        if earlier:
            received = after(received, earlier[-1])
        inner = 0
        pairs = []
        for width in pieces:
            own = unpack(where, received, inner, width)
            pairs.append((own, mirror_pair(own)))
            inner += width
        earlier = [make_rows(*pair, plus_slab, minus_slab) for pair in pairs[:-1]]
        ladder = finish(*pairs[-1], restore, plus_slab, minus_slab, earlier, ladder)
    return ladder


def solution(mesh):
    placed = (
        P("tiles", None, "pair"),
        P("tiles", None, None, None),
        P("tiles", None, None, None),
        P("pair"),
        P(),
        P(),
    )
    return jax.shard_map(
        body, mesh=mesh, in_specs=placed, out_specs=P("pair", "tiles"), check_vma=False
    )
```

```python
import functools

import jax
import jax.numpy as jnp
from jax import lax
from jax.experimental import pallas as pl
from jax.experimental.pallas import tpu as pltpu
from jax.sharding import PartitionSpec as P

CHUNKS = ((512, 128), (256, 128))
BLOCK = 512
VMEM_LIMIT = 20 * 1024 * 1024


def mirror_pair(x):
    return lax.ppermute(x, "pair", [(i, i ^ 1) for i in range(lax.axis_size("pair"))])


def whole(count):
    return [pl.BlockSpec(memory_space=pltpu.VMEM)] * count


def scalars():
    return [pl.BlockSpec(memory_space=pltpu.SMEM)]


def params():
    return pltpu.CompilerParams(vmem_limit_bytes=VMEM_LIMIT)


def pack_kernel(table_ref, tiles_ref, out_ref):
    for k in range(out_ref.shape[0]):
        out_ref[k] = tiles_ref[table_ref[k]]


def pack(table, tiles):
    count = table.shape[0]
    return pl.pallas_call(
        pack_kernel,
        out_shape=jax.ShapeDtypeStruct((count,) + tiles.shape[1:], tiles.dtype),
        in_specs=scalars() + whole(1),
        out_specs=whole(1)[0],
        compiler_params=params(),
    )(table, tiles)


def window_kernel(begin, where_ref, received_ref, out_ref):
    width = out_ref.shape[2]
    for w in range(out_ref.shape[0]):
        place = where_ref[w]
        tile = received_ref[jnp.maximum(place, 0), :, begin : begin + width]
        out_ref[w] = jnp.where(place >= 0, tile, jnp.zeros_like(tile))


def unpack(where, received, begin, width):
    shape = where.shape + (received.shape[1], width)
    return pl.pallas_call(
        functools.partial(window_kernel, begin),
        out_shape=jax.ShapeDtypeStruct(shape, received.dtype),
        in_specs=scalars() + whole(1),
        out_specs=whole(1)[0],
        compiler_params=params(),
    )(where, received)


def turned_sums(own_ref, mirror_ref):
    slots, tile_width, width = own_ref.shape
    own = own_ref[...].reshape(slots * tile_width, width).astype(jnp.float32)
    mirrored = mirror_ref[...].reshape(slots * tile_width, width).astype(jnp.float32)
    plus = (own + mirrored).astype(jnp.bfloat16).T
    minus = (own - mirrored).astype(jnp.bfloat16).T
    return plus, minus


def product(plus, minus, plus_ref, minus_ref, across):
    depth = plus.shape[1]
    block = across.stop - across.start
    total = jnp.dot(
        plus, plus_ref[:, :, across].reshape(depth, block), preferred_element_type=jnp.float32
    )
    total = total + jnp.dot(
        minus, minus_ref[:, :, across].reshape(depth, block), preferred_element_type=jnp.float32
    )
    return (0.5 * total).astype(jnp.bfloat16)


def rows_kernel(own_ref, mirror_ref, plus_ref, minus_ref, out_ref):
    plus, minus = turned_sums(own_ref, mirror_ref)
    for begin in range(0, out_ref.shape[1], BLOCK):
        across = slice(begin, begin + BLOCK)
        out_ref[:, across] = product(plus, minus, plus_ref, minus_ref, across)


def cost(own, columns, more=0):
    depth = own.shape[0] * own.shape[1]
    return pl.CostEstimate(
        flops=4 * depth * own.shape[2] * columns + more,
        bytes_accessed=8 * depth * columns,
        transcendentals=0,
    )


def make_rows(own, mirrored, plus_slab, minus_slab):
    columns = plus_slab.shape[2]
    return pl.pallas_call(
        rows_kernel,
        out_shape=jax.ShapeDtypeStruct((own.shape[2], columns), jnp.bfloat16),
        in_specs=whole(4),
        out_specs=whole(1)[0],
        compiler_params=params(),
        cost_estimate=cost(own, columns),
    )(own, mirrored, plus_slab, minus_slab)


def finish_kernel(earlier, based, last, *refs):
    own_ref, mirror_ref, restore_ref, plus_ref, minus_ref = refs[:5]
    earlier_refs = refs[5 : 5 + earlier]
    base_ref = refs[5 + earlier] if based else None
    refs = refs[5 + earlier + based :]
    plus, minus = turned_sums(own_ref, mirror_ref)
    stores = []
    for b in range(plus_ref.shape[2] // BLOCK):
        across = slice(b * BLOCK, b * BLOCK + BLOCK)
        parts = [ref[:, across] for ref in earlier_refs]
        parts.append(product(plus, minus, plus_ref, minus_ref, across))
        rows = parts[0] if len(parts) == 1 else jnp.concatenate(parts, axis=0)
        ladder = jnp.dot(restore_ref[...], rows, preferred_element_type=jnp.float32)
        if based:
            ladder = ladder + base_ref[:, across].astype(jnp.float32)
        if last:
            out_hbm, held, sems = refs
            held[b] = ladder.astype(held.dtype)
            store = pltpu.make_async_copy(held.at[b], out_hbm.at[:, across], sems.at[b])
            store.start()
            stores.append(store)
        else:
            refs[0][:, across] = ladder.astype(jnp.bfloat16)
    for store in stores:
        store.wait()


def finish(own, mirrored, restore, plus_slab, minus_slab, earlier, base, last):
    columns = plus_slab.shape[2]
    rows = restore.shape[0]
    blocks = columns // BLOCK
    operands = [own, mirrored, restore, plus_slab, minus_slab, *earlier]
    if base is not None:
        operands.append(base)
    held = [pltpu.VMEM((blocks, rows, BLOCK), jnp.bfloat16), pltpu.SemaphoreType.DMA((blocks,))]
    return pl.pallas_call(
        functools.partial(finish_kernel, len(earlier), base is not None, last),
        out_shape=jax.ShapeDtypeStruct((rows, columns), jnp.bfloat16),
        in_specs=whole(len(operands)),
        out_specs=pl.BlockSpec(memory_space=pltpu.HBM if last else pltpu.VMEM),
        scratch_shapes=held if last else [],
        compiler_params=params(),
        cost_estimate=cost(own, columns, 2 * rows * restore.shape[1] * columns),
    )(*operands)


def pin_kernel(slab_ref, out_ref, sem):
    copy = pltpu.make_async_copy(slab_ref, out_ref, sem)
    copy.start()
    copy.wait()


def pin(slab):
    return pl.pallas_call(
        pin_kernel,
        out_shape=pltpu.VMEM(slab.shape, slab.dtype),
        in_specs=[pl.BlockSpec(memory_space=pltpu.HBM)],
        out_specs=pl.BlockSpec(memory_space=pltpu.VMEM),
        scratch_shapes=[pltpu.SemaphoreType.DMA],
        compiler_params=params(),
    )(slab)


def route_plan(win_tile, win_count, me):
    slots = win_tile.shape[1]
    position = jnp.arange(slots)
    sources = win_tile >> 5
    mine = (sources == me) & (position[None, :] < win_count[:, None])
    coded = position[None, :] * 32 + (win_tile & 31)
    first = jnp.min(jnp.where(mine, coded, 1 << 20), axis=1) & 31
    last = jnp.maximum(jnp.max(jnp.where(mine, coded, -1), axis=1), 0) & 31
    send = jnp.stack([first, last], axis=1).reshape(-1)
    own = lax.dynamic_index_in_dim(sources, me, 0, keepdims=False)
    living = position < lax.dynamic_index_in_dim(win_count, me, 0, keepdims=False)
    earlier = (
        (own[:, None] == own[None, :])
        & living[None, :]
        & (position[None, :] < position[:, None])
    )
    rank = jnp.any(earlier, axis=1).astype(jnp.int32)
    return send, jnp.where(living, own * 2 + rank, -1)


def after(value, *others):
    return lax.optimization_barrier((value,) + others)[0]


def body(t2, v_plus, v_minus, partner, win_tile, win_count):
    tiles, tile_width, rows = t2.shape
    me = lax.axis_index("tiles")
    odd = lax.axis_index("pair") % 2 == 1
    index = jnp.arange(rows)
    order = jnp.where(odd, partner, index)
    send, where = route_plan(win_tile, win_count, me)
    flat = t2.reshape(tiles * tile_width, rows)
    begin = 0
    chunks, restores = [], []
    for pieces in CHUNKS:
        width = sum(pieces)
        select = (order[:, None] == index[None, begin : begin + width]).astype(jnp.bfloat16)
        chunk = jnp.dot(flat, select, preferred_element_type=jnp.float32).astype(jnp.bfloat16)
        chunks.append(chunk.reshape(tiles, tile_width, width))
        restores.append(select)
        begin += width
    landed = [lax.all_to_all(pack(send, chunks[0]), "tiles", 0, 0, tiled=True)]
    early = tuple(restores) + (where,) + tuple(chunks[1:])
    plus_slab = pin(after(v_plus[0], *early))
    minus_slab = pin(after(v_minus[0], *early))
    for chunk in chunks[1:]:
        outgoing = pack(send, after(chunk, plus_slab, minus_slab))
        outgoing = after(outgoing, landed[-1])
        landed.append(lax.all_to_all(outgoing, "tiles", 0, 0, tiled=True))
    ladder = None
    ladder = None
    begin = 0
    earlier = []
    for pieces, received, restore in zip(CHUNKS, landed, restores, strict=True):
        if earlier:
            received = after(received, earlier[-1])
        begin += restore.shape[1]
        inner = 0
        pairs = []
        for width in pieces:
            own = unpack(where, received, inner, width)
            pairs.append((own, mirror_pair(own)))
            inner += width
        earlier = [make_rows(*pair, plus_slab, minus_slab) for pair in pairs[:-1]]
        ladder = finish(*pairs[-1], restore, plus_slab, minus_slab, earlier, ladder, begin == rows)
    return ladder


def solution(mesh):
    placed = (
        P("tiles", None, "pair"),
        P("tiles", None, None, None),
        P("tiles", None, None, None),
        P("pair"),
        P(),
        P(),
    )
    return jax.shard_map(
        body, mesh=mesh, in_specs=placed, out_specs=P("pair", "tiles"), check_vma=False
    )
```

```python
import functools

import jax
import jax.numpy as jnp
from jax import lax
from jax.experimental import pallas as pl
from jax.experimental.pallas import tpu as pltpu
from jax.sharding import PartitionSpec as P

CHUNKS = ((384, 256), (256, 128))
BLOCK = 512
VMEM_LIMIT = 20 * 1024 * 1024


def mirror_pair(x):
    return lax.ppermute(x, "pair", [(i, i ^ 1) for i in range(lax.axis_size("pair"))])


def whole(count):
    return [pl.BlockSpec(memory_space=pltpu.VMEM)] * count


def scalars():
    return [pl.BlockSpec(memory_space=pltpu.SMEM)]


def params():
    return pltpu.CompilerParams(vmem_limit_bytes=VMEM_LIMIT)


def pack_kernel(table_ref, tiles_ref, out_ref):
    for k in range(out_ref.shape[0]):
        out_ref[k] = tiles_ref[table_ref[k]]


def pack(table, tiles):
    count = table.shape[0]
    return pl.pallas_call(
        pack_kernel,
        out_shape=jax.ShapeDtypeStruct((count,) + tiles.shape[1:], tiles.dtype),
        in_specs=scalars() + whole(1),
        out_specs=whole(1)[0],
        compiler_params=params(),
    )(table, tiles)


def window_kernel(begin, where_ref, received_ref, out_ref):
    width = out_ref.shape[2]
    for w in range(out_ref.shape[0]):
        place = where_ref[w]
        tile = received_ref[jnp.maximum(place, 0), :, begin : begin + width]
        out_ref[w] = jnp.where(place >= 0, tile, jnp.zeros_like(tile))


def unpack(where, received, begin, width):
    shape = where.shape + (received.shape[1], width)
    return pl.pallas_call(
        functools.partial(window_kernel, begin),
        out_shape=jax.ShapeDtypeStruct(shape, received.dtype),
        in_specs=scalars() + whole(1),
        out_specs=whole(1)[0],
        compiler_params=params(),
    )(where, received)


def turned_sums(own_ref, mirror_ref):
    slots, tile_width, width = own_ref.shape
    own = own_ref[...].reshape(slots * tile_width, width).astype(jnp.float32)
    mirrored = mirror_ref[...].reshape(slots * tile_width, width).astype(jnp.float32)
    plus = (own + mirrored).astype(jnp.bfloat16).T
    minus = (own - mirrored).astype(jnp.bfloat16).T
    return plus, minus


def product(plus, minus, plus_ref, minus_ref, across):
    depth = plus.shape[1]
    block = across.stop - across.start
    total = jnp.dot(
        plus, plus_ref[:, :, across].reshape(depth, block), preferred_element_type=jnp.float32
    )
    total = total + jnp.dot(
        minus, minus_ref[:, :, across].reshape(depth, block), preferred_element_type=jnp.float32
    )
    return (0.5 * total).astype(jnp.bfloat16)


def rows_kernel(own_ref, mirror_ref, plus_ref, minus_ref, out_ref):
    plus, minus = turned_sums(own_ref, mirror_ref)
    for begin in range(0, out_ref.shape[1], BLOCK):
        across = slice(begin, begin + BLOCK)
        out_ref[:, across] = product(plus, minus, plus_ref, minus_ref, across)


def cost(own, columns, more=0):
    depth = own.shape[0] * own.shape[1]
    return pl.CostEstimate(
        flops=4 * depth * own.shape[2] * columns + more,
        bytes_accessed=8 * depth * columns,
        transcendentals=0,
    )


def make_rows(own, mirrored, plus_slab, minus_slab):
    columns = plus_slab.shape[2]
    return pl.pallas_call(
        rows_kernel,
        out_shape=jax.ShapeDtypeStruct((own.shape[2], columns), jnp.bfloat16),
        in_specs=whole(4),
        out_specs=whole(1)[0],
        compiler_params=params(),
        cost_estimate=cost(own, columns),
    )(own, mirrored, plus_slab, minus_slab)


def finish_kernel(earlier, based, last, *refs):
    own_ref, mirror_ref, restore_ref, plus_ref, minus_ref = refs[:5]
    earlier_refs = refs[5 : 5 + earlier]
    base_ref = refs[5 + earlier] if based else None
    refs = refs[5 + earlier + based :]
    plus, minus = turned_sums(own_ref, mirror_ref)
    stores = []
    for b in range(plus_ref.shape[2] // BLOCK):
        across = slice(b * BLOCK, b * BLOCK + BLOCK)
        parts = [ref[:, across] for ref in earlier_refs]
        parts.append(product(plus, minus, plus_ref, minus_ref, across))
        rows = parts[0] if len(parts) == 1 else jnp.concatenate(parts, axis=0)
        ladder = jnp.dot(restore_ref[...], rows, preferred_element_type=jnp.float32)
        if based:
            ladder = ladder + base_ref[:, across].astype(jnp.float32)
        if last:
            out_hbm, held, sems = refs
            held[b] = ladder.astype(held.dtype)
            store = pltpu.make_async_copy(held.at[b], out_hbm.at[:, across], sems.at[b])
            store.start()
            stores.append(store)
        else:
            refs[0][:, across] = ladder.astype(jnp.bfloat16)
    for store in stores:
        store.wait()


def finish(own, mirrored, restore, plus_slab, minus_slab, earlier, base, last):
    columns = plus_slab.shape[2]
    rows = restore.shape[0]
    blocks = columns // BLOCK
    operands = [own, mirrored, restore, plus_slab, minus_slab, *earlier]
    if base is not None:
        operands.append(base)
    held = [pltpu.VMEM((blocks, rows, BLOCK), jnp.bfloat16), pltpu.SemaphoreType.DMA((blocks,))]
    return pl.pallas_call(
        functools.partial(finish_kernel, len(earlier), base is not None, last),
        out_shape=jax.ShapeDtypeStruct((rows, columns), jnp.bfloat16),
        in_specs=whole(len(operands)),
        out_specs=pl.BlockSpec(memory_space=pltpu.HBM if last else pltpu.VMEM),
        scratch_shapes=held if last else [],
        compiler_params=params(),
        cost_estimate=cost(own, columns, 2 * rows * restore.shape[1] * columns),
    )(*operands)


def pin_kernel(slab_ref, out_ref, sem):
    copy = pltpu.make_async_copy(slab_ref, out_ref, sem)
    copy.start()
    copy.wait()


def pin(slab):
    return pl.pallas_call(
        pin_kernel,
        out_shape=pltpu.VMEM(slab.shape, slab.dtype),
        in_specs=[pl.BlockSpec(memory_space=pltpu.HBM)],
        out_specs=pl.BlockSpec(memory_space=pltpu.VMEM),
        scratch_shapes=[pltpu.SemaphoreType.DMA],
        compiler_params=params(),
    )(slab)


def route_plan(win_tile, win_count, me):
    slots = win_tile.shape[1]
    position = jnp.arange(slots)
    sources = win_tile >> 5
    mine = (sources == me) & (position[None, :] < win_count[:, None])
    coded = position[None, :] * 32 + (win_tile & 31)
    first = jnp.min(jnp.where(mine, coded, 1 << 20), axis=1) & 31
    last = jnp.maximum(jnp.max(jnp.where(mine, coded, -1), axis=1), 0) & 31
    send = jnp.stack([first, last], axis=1).reshape(-1)
    own = lax.dynamic_index_in_dim(sources, me, 0, keepdims=False)
    living = position < lax.dynamic_index_in_dim(win_count, me, 0, keepdims=False)
    earlier = (
        (own[:, None] == own[None, :])
        & living[None, :]
        & (position[None, :] < position[:, None])
    )
    rank = jnp.any(earlier, axis=1).astype(jnp.int32)
    return send, jnp.where(living, own * 2 + rank, -1)


def after(value, *others):
    return lax.optimization_barrier((value,) + others)[0]


def body(t2, v_plus, v_minus, partner, win_tile, win_count):
    tiles, tile_width, rows = t2.shape
    me = lax.axis_index("tiles")
    odd = lax.axis_index("pair") % 2 == 1
    index = jnp.arange(rows)
    order = jnp.where(odd, partner, index)
    send, where = route_plan(win_tile, win_count, me)
    flat = t2.reshape(tiles * tile_width, rows)
    begin = 0
    chunks, restores = [], []
    for pieces in CHUNKS:
        width = sum(pieces)
        select = (order[:, None] == index[None, begin : begin + width]).astype(jnp.bfloat16)
        chunk = jnp.dot(flat, select, preferred_element_type=jnp.float32).astype(jnp.bfloat16)
        chunks.append(chunk.reshape(tiles, tile_width, width))
        restores.append(select)
        begin += width
    landed = [lax.all_to_all(pack(send, chunks[0]), "tiles", 0, 0, tiled=True)]
    early = tuple(restores) + (where,) + tuple(chunks[1:])
    plus_slab = pin(after(v_plus[0], *early))
    minus_slab = pin(after(v_minus[0], *early))
    for chunk in chunks[1:]:
        outgoing = pack(send, after(chunk, plus_slab, minus_slab))
        outgoing = after(outgoing, landed[-1])
        landed.append(lax.all_to_all(outgoing, "tiles", 0, 0, tiled=True))
    ladder = None
    ladder = None
    begin = 0
    earlier = []
    for pieces, received, restore in zip(CHUNKS, landed, restores, strict=True):
        if earlier:
            received = after(received, earlier[-1])
        begin += restore.shape[1]
        inner = 0
        pairs = []
        for width in pieces:
            own = unpack(where, received, inner, width)
            pairs.append((own, mirror_pair(own)))
            inner += width
        earlier = [make_rows(*pair, plus_slab, minus_slab) for pair in pairs[:-1]]
        ladder = finish(*pairs[-1], restore, plus_slab, minus_slab, earlier, ladder, begin == rows)
    return ladder


def solution(mesh):
    placed = (
        P("tiles", None, "pair"),
        P("tiles", None, None, None),
        P("tiles", None, None, None),
        P("pair"),
        P(),
        P(),
    )
    return jax.shard_map(
        body, mesh=mesh, in_specs=placed, out_specs=P("pair", "tiles"), check_vma=False
    )
```

```python
import functools

import jax
import jax.numpy as jnp
from jax import lax
from jax.experimental import pallas as pl
from jax.experimental.pallas import tpu as pltpu
from jax.sharding import PartitionSpec as P

CHUNKS = ((512, 128), (256, 128))
BLOCK = 512
VMEM_LIMIT = 20 * 1024 * 1024


def mirror_pair(x):
    return lax.ppermute(x, "pair", [(i, i ^ 1) for i in range(lax.axis_size("pair"))])


def whole(count):
    return [pl.BlockSpec(memory_space=pltpu.VMEM)] * count


def scalars():
    return [pl.BlockSpec(memory_space=pltpu.SMEM)]


def params():
    return pltpu.CompilerParams(vmem_limit_bytes=VMEM_LIMIT)


def pack_kernel(first_ref, last_ref, tiles_ref, out_ref):
    for k in range(first_ref.shape[0]):
        out_ref[2 * k] = tiles_ref[first_ref[k]]
        out_ref[2 * k + 1] = tiles_ref[last_ref[k]]


def pack(tables, tiles):
    count = 2 * tables[0].shape[0]
    return pl.pallas_call(
        pack_kernel,
        out_shape=jax.ShapeDtypeStruct((count,) + tiles.shape[1:], tiles.dtype),
        in_specs=scalars() * 2 + whole(1),
        out_specs=whole(1)[0],
        compiler_params=params(),
    )(*tables, tiles)


def window_kernel(begin, where_ref, received_ref, out_ref):
    width = out_ref.shape[2]
    for w in range(out_ref.shape[0]):
        place = where_ref[w]
        tile = received_ref[jnp.maximum(place, 0), :, begin : begin + width]
        out_ref[w] = jnp.where(place >= 0, tile, jnp.zeros_like(tile))


def unpack(where, received, begin, width):
    shape = where.shape + (received.shape[1], width)
    return pl.pallas_call(
        functools.partial(window_kernel, begin),
        out_shape=jax.ShapeDtypeStruct(shape, received.dtype),
        in_specs=scalars() + whole(1),
        out_specs=whole(1)[0],
        compiler_params=params(),
    )(where, received)


def turned_sums(own_ref, mirror_ref):
    slots, tile_width, width = own_ref.shape
    own = own_ref[...].reshape(slots * tile_width, width).astype(jnp.float32)
    mirrored = mirror_ref[...].reshape(slots * tile_width, width).astype(jnp.float32)
    plus = (own + mirrored).astype(jnp.bfloat16).T
    minus = (own - mirrored).astype(jnp.bfloat16).T
    return plus, minus


def product(plus, minus, plus_ref, minus_ref, across):
    depth = plus.shape[1]
    block = across.stop - across.start
    total = jnp.dot(
        plus, plus_ref[:, :, across].reshape(depth, block), preferred_element_type=jnp.float32
    )
    total = total + jnp.dot(
        minus, minus_ref[:, :, across].reshape(depth, block), preferred_element_type=jnp.float32
    )
    return (0.5 * total).astype(jnp.bfloat16)


def rows_kernel(own_ref, mirror_ref, plus_ref, minus_ref, out_ref):
    plus, minus = turned_sums(own_ref, mirror_ref)
    for begin in range(0, out_ref.shape[1], BLOCK):
        across = slice(begin, begin + BLOCK)
        out_ref[:, across] = product(plus, minus, plus_ref, minus_ref, across)


def cost(own, columns, more=0):
    depth = own.shape[0] * own.shape[1]
    return pl.CostEstimate(
        flops=4 * depth * own.shape[2] * columns + more,
        bytes_accessed=8 * depth * columns,
        transcendentals=0,
    )


def make_rows(own, mirrored, plus_slab, minus_slab):
    columns = plus_slab.shape[2]
    return pl.pallas_call(
        rows_kernel,
        out_shape=jax.ShapeDtypeStruct((own.shape[2], columns), jnp.bfloat16),
        in_specs=whole(4),
        out_specs=whole(1)[0],
        compiler_params=params(),
        cost_estimate=cost(own, columns),
    )(own, mirrored, plus_slab, minus_slab)


def finish_kernel(earlier, based, last, *refs):
    own_ref, mirror_ref, restore_ref, plus_ref, minus_ref = refs[:5]
    earlier_refs = refs[5 : 5 + earlier]
    base_ref = refs[5 + earlier] if based else None
    refs = refs[5 + earlier + based :]
    plus, minus = turned_sums(own_ref, mirror_ref)
    stores = []
    for b in range(plus_ref.shape[2] // BLOCK):
        across = slice(b * BLOCK, b * BLOCK + BLOCK)
        parts = [ref[:, across] for ref in earlier_refs]
        parts.append(product(plus, minus, plus_ref, minus_ref, across))
        rows = parts[0] if len(parts) == 1 else jnp.concatenate(parts, axis=0)
        ladder = jnp.dot(restore_ref[...], rows, preferred_element_type=jnp.float32)
        if based:
            ladder = ladder + base_ref[:, across].astype(jnp.float32)
        if last:
            out_hbm, held, sems = refs
            held[b] = ladder.astype(held.dtype)
            store = pltpu.make_async_copy(held.at[b], out_hbm.at[:, across], sems.at[b])
            store.start()
            stores.append(store)
        else:
            refs[0][:, across] = ladder.astype(jnp.bfloat16)
    for store in stores:
        store.wait()


def finish(own, mirrored, restore, plus_slab, minus_slab, earlier, base, last):
    columns = plus_slab.shape[2]
    rows = restore.shape[0]
    blocks = columns // BLOCK
    operands = [own, mirrored, restore, plus_slab, minus_slab, *earlier]
    if base is not None:
        operands.append(base)
    held = [pltpu.VMEM((blocks, rows, BLOCK), jnp.bfloat16), pltpu.SemaphoreType.DMA((blocks,))]
    return pl.pallas_call(
        functools.partial(finish_kernel, len(earlier), base is not None, last),
        out_shape=jax.ShapeDtypeStruct((rows, columns), jnp.bfloat16),
        in_specs=whole(len(operands)),
        out_specs=pl.BlockSpec(memory_space=pltpu.HBM if last else pltpu.VMEM),
        scratch_shapes=held if last else [],
        compiler_params=params(),
        cost_estimate=cost(own, columns, 2 * rows * restore.shape[1] * columns),
    )(*operands)


def pin_kernel(slab_ref, out_ref, sem):
    copy = pltpu.make_async_copy(slab_ref, out_ref, sem)
    copy.start()
    copy.wait()


def pin(slab):
    return pl.pallas_call(
        pin_kernel,
        out_shape=pltpu.VMEM(slab.shape, slab.dtype),
        in_specs=[pl.BlockSpec(memory_space=pltpu.HBM)],
        out_specs=pl.BlockSpec(memory_space=pltpu.VMEM),
        scratch_shapes=[pltpu.SemaphoreType.DMA],
        compiler_params=params(),
    )(slab)


def route_plan(win_tile, win_count, me):
    slots = win_tile.shape[1]
    position = jnp.arange(slots)
    sources = win_tile >> 5
    mine = (sources == me) & (position[None, :] < win_count[:, None])
    coded = position[None, :] * 32 + (win_tile & 31)
    first = jnp.min(jnp.where(mine, coded, 1 << 20), axis=1) & 31
    last = jnp.maximum(jnp.max(jnp.where(mine, coded, -1), axis=1), 0) & 31
    send = first, last
    own = lax.dynamic_index_in_dim(sources, me, 0, keepdims=False)
    living = position < lax.dynamic_index_in_dim(win_count, me, 0, keepdims=False)
    earlier = (
        (own[:, None] == own[None, :])
        & living[None, :]
        & (position[None, :] < position[:, None])
    )
    rank = jnp.any(earlier, axis=1).astype(jnp.int32)
    return send, jnp.where(living, own * 2 + rank, -1)


def after(value, *others):
    return lax.optimization_barrier((value,) + others)[0]


def body(t2, v_plus, v_minus, partner, win_tile, win_count):
    tiles, tile_width, rows = t2.shape
    me = lax.axis_index("tiles")
    odd = lax.axis_index("pair") % 2 == 1
    index = jnp.arange(rows)
    order = jnp.where(odd, partner, index)
    send, where = route_plan(win_tile, win_count, me)
    flat = t2.reshape(tiles * tile_width, rows)
    begin = 0
    chunks, restores = [], []
    for pieces in CHUNKS:
        width = sum(pieces)
        select = (order[:, None] == index[None, begin : begin + width]).astype(jnp.bfloat16)
        chunk = jnp.dot(flat, select, preferred_element_type=jnp.float32).astype(jnp.bfloat16)
        chunks.append(chunk.reshape(tiles, tile_width, width))
        restores.append(select)
        begin += width
    landed = [lax.all_to_all(pack(send, chunks[0]), "tiles", 0, 0, tiled=True)]
    early = tuple(restores) + (where,) + tuple(chunks[1:])
    plus_slab = pin(after(v_plus[0], *early))
    minus_slab = pin(after(v_minus[0], *early))
    for chunk in chunks[1:]:
        outgoing = pack(send, after(chunk, plus_slab, minus_slab))
        outgoing = after(outgoing, landed[-1])
        landed.append(lax.all_to_all(outgoing, "tiles", 0, 0, tiled=True))
    ladder = None
    ladder = None
    begin = 0
    earlier = []
    for pieces, received, restore in zip(CHUNKS, landed, restores, strict=True):
        if earlier:
            received = after(received, earlier[-1])
        begin += restore.shape[1]
        inner = 0
        pairs = []
        for width in pieces:
            own = unpack(where, received, inner, width)
            pairs.append((own, mirror_pair(own)))
            inner += width
        earlier = [make_rows(*pair, plus_slab, minus_slab) for pair in pairs[:-1]]
        ladder = finish(*pairs[-1], restore, plus_slab, minus_slab, earlier, ladder, begin == rows)
    return ladder


def solution(mesh):
    placed = (
        P("tiles", None, "pair"),
        P("tiles", None, None, None),
        P("tiles", None, None, None),
        P("pair"),
        P(),
        P(),
    )
    return jax.shard_map(
        body, mesh=mesh, in_specs=placed, out_specs=P("pair", "tiles"), check_vma=False
    )
```
